256 devices in a mesh: section: 4 (over z_hi, core), mp: 64 (over y, x, z_lo).
Axes of the slice: x: 4, y: 4, z: 8 (z_hi: 2, z_lo: 4; z = z_hi * 4 + z_lo), core: 2. Of those that a mesh axis runs over, the one named last changes fastest.
Arguments:
- activations: bfloat16 [4, 512, 4096], P('section', 'mp'), may hold values from -24 to 24
- enc_weight: bfloat16 [4, 4096, 32768], P('section', None, 'mp'), may hold values from -0.046875 to 0.046875
- enc_bias: float32 [32768], P('mp'), may hold values from -4 to 4
- dec_weight: bfloat16 [32768, 4, 4096], P('mp', 'section'), may hold values from -0.77339804 to 0.77339804
- dec_bias: float32 [4, 4096], P('section'), may hold values from -3 to 3
Outputs:
- loss: float32 [], replicated
- grad_dec: bfloat16 [32768, 4, 4096], P('mp', 'section')
- grad_bias: float32 [4, 4096], P('section', 'mp')
The draws below stay inside these ranges and needn't reach their ends.
All inputs are finite; a program needn't handle non-finite values.
Results may differ from the reference program's by a relative error of at most 0.009.
Values may be sent and summed in bfloat16 or wider, within the bound.
No kernel may reach another device: no remote copies, remote signals or barrier semaphores. Data moves between devices by JAX's collectives and lax.ppermute only.
A program may use at most 64 MiB of HBM per device.

```python
import math
import jax
import jax.numpy as jnp
from jax import lax

D = 4096
LAYERS = 4
HID = 32768
TOKENS = 512


def draw_activations(key, part):
    keys = jax.random.split(jax.random.fold_in(key, 11), 2)
    position = jnp.arange(TOKENS, dtype=jnp.float32)
    ramp = 1.0 + 2.0 * position / max(TOKENS - 1, 1)
    jitter = jnp.exp(jax.random.uniform(keys[1], (LAYERS, TOKENS, 1), jnp.float32, -0.4, 0.4))
    scale_rows = ramp[None, :, None] * jitter
    base = jax.random.normal(keys[0], (LAYERS, TOKENS, D), jnp.float32)
    return jnp.clip(base * scale_rows, -24.0, 24.0).astype(jnp.bfloat16)


def draw_dec_weight(key, part):
    keys = jax.random.split(jax.random.fold_in(key, 23), 4)
    row_scale = jnp.exp(jax.random.uniform(keys[1], (HID, 1, 1), jnp.float32, math.log(0.3), math.log(3.0)))
    col_scale = jnp.exp(jax.random.uniform(keys[2], (1, 1, D), jnp.float32, math.log(0.3), math.log(3.0)))
    level = jnp.arange(LAYERS, dtype=jnp.float32)
    layer_ramp = 0.5 + level / max(LAYERS - 1, 1)
    layer_jitter = jnp.exp(jax.random.uniform(keys[3], (HID, LAYERS, 1), jnp.float32, -0.5, 0.5))
    layer_scale = layer_ramp[None, :, None] * layer_jitter
    base = jnp.clip(jax.random.normal(keys[0], (HID, LAYERS, D), jnp.float32), -6.0, 6.0)
    return (base * row_scale * col_scale * layer_scale / math.sqrt(HID)).astype(jnp.bfloat16)


def level_of(own_key, shape, pieces, smallest, high):
    gain, own = 1.0, jax.random.fold_in(own_key, 6)
    for axis_at, shards_of in pieces:
        steps = jnp.exp(jax.random.uniform(jax.random.fold_in(own, axis_at), (shards_of,), jnp.float32, smallest / len(pieces), high / len(pieces)))
        gain = gain * jnp.repeat(steps, shape[axis_at] // shards_of).reshape([-1 if axis == axis_at else 1 for axis in range(len(shape))])
    return gain


def centred(rng, shape, spread, limit, cuts=(), held_as=jnp.bfloat16):
    level = level_of(rng, shape, cuts, -0.22, 0.18) if cuts else 1.0
    drawn = jax.random.normal(rng, shape, jnp.float32) * spread * level
    return jnp.minimum(jnp.maximum(drawn, -limit), limit).astype(held_as)


def setup_inputs(seed: int = 0) -> dict:
    streams_of = jax.random.split(jax.random.key(seed), 6)
    activations = draw_activations(jax.random.fold_in(streams_of[5], 71), 0)
    enc_weight = centred(streams_of[1], (LAYERS, D, HID), (LAYERS * D) ** -0.5, 0.046875, ((0, 4), (2, 64)))
    enc_bias = centred(streams_of[2], (HID,), 1.0, 4.0, ((0, 64),), jnp.float32)
    dec_weight = draw_dec_weight(jax.random.fold_in(streams_of[5], 71), 0)
    dec_bias = centred(streams_of[4], (LAYERS, D), 0.5, 3.0, ((0, 4),), jnp.float32)
    return dict(activations=activations, enc_weight=enc_weight, enc_bias=enc_bias, dec_weight=dec_weight, dec_bias=dec_bias)


penalty_weight = 2.0

def reference(activations, enc_weight, enc_bias, dec_weight, dec_bias):
    token_count = activations.shape[1]
    pre_sum = jnp.zeros((token_count, enc_weight.shape[2]), jnp.float32) + enc_bias[None, :]
    for layer in range(LAYERS):
        pre_sum = pre_sum + jnp.dot(activations[layer], enc_weight[layer], preferred_element_type=jnp.float32)
    latents = jnp.maximum(pre_sum, 0.0).astype(jnp.bfloat16)
    latent_sum = lax.optimization_barrier(jnp.sum(latents.astype(jnp.float32), axis=0))
    norm_total = jnp.zeros((enc_weight.shape[2],), jnp.float32)
    square_sum = jnp.zeros((), jnp.float32)
    grad_list = []
    bias_list = []
    for layer in range(LAYERS):
        w_layer = dec_weight[:, layer, :]
        layer_norm = jnp.sqrt(lax.optimization_barrier(jnp.sum(jnp.square(w_layer.astype(jnp.float32)), axis=1)) + 1e-06)
        norm_total = norm_total + layer_norm
        recon = jnp.dot(latents, w_layer, preferred_element_type=jnp.float32) + dec_bias[layer][None, :]
        error = recon - activations[layer].astype(jnp.float32)
        square_sum = square_sum + jnp.sum(error * error)
        scaled = 2.0 * error / token_count
        grad_rec = scaled.astype(jnp.bfloat16)
        bias_list.append(lax.optimization_barrier(jnp.sum(scaled, axis=0)))
        grad_sum = jnp.dot(latents.T, grad_rec, preferred_element_type=jnp.float32)
        coef = penalty_weight * latent_sum / token_count / layer_norm
        grad_list.append((grad_sum + coef[:, None] * w_layer.astype(jnp.float32)).astype(jnp.bfloat16))
    penalty_part = penalty_weight / token_count * jnp.sum(latents.astype(jnp.float32) * norm_total[None, :])
    loss = square_sum / token_count + penalty_part
    grad_dec = jnp.stack(grad_list, axis=1)
    grad_bias = jnp.stack(bias_list, axis=0)
    return (loss, grad_dec, grad_bias)
```

```python
import jax
import jax.numpy as jnp
from jax import lax
from jax.sharding import Mesh, PartitionSpec as P

penalty_weight = 2.0
SIDE = 4
bf16, f32 = jnp.bfloat16, jnp.float32


def shift(value, axis, step):
    return lax.ppermute(value, axis, [(i, (i + step) % SIDE) for i in range(SIDE)])


def swap(value, axis):
    return lax.ppermute(value, axis, [(0, 1), (1, 0)])


def gather(value, axis):
    return [value] + [shift(value, axis, r) for r in range(1, SIDE)]


def scatter_sum(blocks, axis):
    total = blocks[0]
    for r in range(1, SIDE):
        total = total + shift(blocks[r].astype(bf16), axis, -r).astype(f32)
    return total


def gather_rows(rows):
    z = gather(rows, "z")
    a = jnp.concatenate(z[:2], axis=0)
    b = jnp.concatenate(z[2:], axis=0)
    a = jnp.concatenate(gather(a, "x"), axis=0)
    b = jnp.concatenate(gather(b, "y"), axis=0)
    return gather(a, "y"), gather(b, "x")


def scatter_rows(chunks_a, chunks_b):
    a = scatter_sum(chunks_a, "y")
    b = scatter_sum(chunks_b, "x")
    a = scatter_sum([a[16 * i : 16 * i + 16] for i in range(SIDE)], "x")
    b = scatter_sum([b[16 * i : 16 * i + 16] for i in range(SIDE)], "y")
    return scatter_sum([a[:8], a[8:], b[:8], b[8:]], "z")


def section_latents(part, enc_bias):
    half = part.shape[0] // 2
    first = lax.axis_index("core") == 0
    keep = jnp.where(first, part[:half], part[half:])
    give = jnp.where(first, part[half:], part[:half]).astype(bf16)
    keep = keep + swap(give, "core").astype(f32)
    keep = keep + swap(keep.astype(bf16), "zh").astype(f32)
    mine = jnp.maximum(keep + enc_bias[None, :], 0.0).astype(bf16)
    other = swap(mine, "core")
    return jnp.concatenate(
        [jnp.where(first, mine, other), jnp.where(first, other, mine)], axis=0
    )


def sum_all(value):
    for axis in ("z", "x", "y"):
        pair = lax.ppermute(value, axis, [(0, 1), (1, 0), (2, 3), (3, 2)])
        value = value + pair
        pair = lax.ppermute(value, axis, [(0, 3), (3, 0), (1, 2), (2, 1)])
        value = value + pair
    for axis in ("core", "zh"):
        value = value + swap(value, axis)
    return value


def local(activations, enc_weight, enc_bias, dec_weight, dec_bias):
    rows = activations[0]
    chunks_a, chunks_b = gather_rows(rows)
    all_rows = jnp.concatenate(chunks_a + chunks_b, axis=0)
    token_count = all_rows.shape[0]
    partial_value = jnp.dot(all_rows, enc_weight[0], preferred_element_type=f32)
    w_dec = dec_weight[:, 0, :]
    layer_norm = jnp.sqrt(jnp.sum(jnp.square(w_dec.astype(f32)), axis=1) + 1e-06)
    latents = section_latents(partial_value, enc_bias)
    latent_sum = jnp.sum(latents.astype(f32), axis=0)
    penalty_part = penalty_weight / token_count * jnp.sum(latent_sum * layer_norm)
    coef = penalty_weight * latent_sum / token_count / layer_norm
    recon = jnp.dot(latents, w_dec, preferred_element_type=f32)
    size = token_count // 8
    chunks = [recon[size * i : size * i + size] for i in range(8)]
    recon_rows = scatter_rows(chunks[:4], chunks[4:])
    error_rows = recon_rows + dec_bias[0][None, :] - rows.astype(f32)
    square_sum = jnp.sum(error_rows * error_rows)
    loss = sum_all(jnp.reshape(square_sum / token_count + penalty_part, (1,)))[0]
    grad_rec = (2.0 * error_rows / token_count).astype(bf16)
    grads_a, grads_b = gather_rows(grad_rec)
    all_grads = jnp.concatenate(grads_a + grads_b, axis=0)
    place = (lax.axis_index("y") * SIDE + lax.axis_index("x")) * SIDE + lax.axis_index("z")
    width = all_grads.shape[1] // SIDE**3
    own = lax.dynamic_slice_in_dim(all_grads, place * width, width, axis=1)
    grad_bias = jnp.sum(own.astype(f32), axis=0, keepdims=True)
    grad_sum = lax.dot_general(
        latents, all_grads, (((0,), (0,)), ((), ())), preferred_element_type=f32
    )
    grad_dec = (grad_sum + coef[:, None] * w_dec.astype(f32)).astype(bf16)[:, None, :]
    return (loss, grad_dec, grad_bias)


def solution(mesh):
    grid = Mesh(
        mesh.devices.reshape(2, 2, SIDE, SIDE, SIDE), ("zh", "core", "y", "x", "z")
    )
    section, mp = ("zh", "core"), ("y", "x", "z")
    in_specs = (
        P(section, mp, None),
        P(section, None, mp),
        P(mp),
        P(mp, section, None),
        P(section, None),
    )
    out_specs = (P(), P(mp, section, None), P(section, mp))
    return jax.shard_map(local, mesh=grid, in_specs=in_specs, out_specs=out_specs, check_vma=False)
```

```python
import jax
import jax.numpy as jnp
from jax import lax
from jax.sharding import Mesh, PartitionSpec as P

penalty_weight = 2.0
SIDE = 4
bf16, f32 = jnp.bfloat16, jnp.float32
together = lax.optimization_barrier


def shift(value, axis, step):
    return lax.ppermute(value, axis, [(i, (i + step) % SIDE) for i in range(SIDE)])


def swap(value, axis):
    return lax.ppermute(value, axis, [(0, 1), (1, 0)])


def gather(value, axis):
    return [value] + [shift(value, axis, r) for r in range(1, SIDE)]


def exchange(blocks, axis):
    return [blocks[0]] + [shift(blocks[r].astype(bf16), axis, -r) for r in range(1, SIDE)]


def add_up(terms):
    total = terms[0]
    for term in terms[1:]:
        total = total + term.astype(f32)
    return total


def join(pieces):
    return jnp.concatenate(pieces, axis=0)


def quarters(block):
    size = block.shape[0] // SIDE
    return [block[size * i : size * i + size] for i in range(SIDE)]


def gather_rows(rows):
    z = together(gather(rows, "z"))
    a, b = together((join(z[:2]), join(z[2:])))
    a, b = together((gather(a, "x"), gather(b, "y")))
    a, b = together((join(a), join(b)))
    return gather(a, "y"), gather(b, "x")


def opposite(chunks, axis):
    block = chunks[2].astype(bf16)
    half = block.shape[0] // 2
    return shift(block[:half], axis, -1), shift(block[half:], axis, 1)


def neighbours(chunks, passed, axis):
    half = chunks[2].shape[0] // 2
    before, after = chunks[1], chunks[3]
    before = join([before[:half] + passed[0].astype(f32), before[half:]])
    after = join([after[:half], after[half:] + passed[1].astype(f32)])
    return shift(before.astype(bf16), axis, -1), shift(after.astype(bf16), axis, 1)


def scatter_rows(chunks_a, chunks_b):
    a, b = together((opposite(chunks_a, "y"), opposite(chunks_b, "x")))
    a, b = together((neighbours(chunks_a, a, "y"), neighbours(chunks_b, b, "x")))
    a, b = together((add_up([chunks_a[0], *a]), add_up([chunks_b[0], *b])))
    a, b = together((exchange(quarters(a), "x"), exchange(quarters(b), "y")))
    a, b = together((add_up(a), add_up(b)))
    return add_up(together(exchange([a[:8], a[8:], b[:8], b[8:]], "z")))


def section_latents(part, enc_bias):
    half = part.shape[0] // 2
    first = lax.axis_index("core") == 0
    keep = jnp.where(first, part[:half], part[half:])
    give = jnp.where(first, part[half:], part[:half]).astype(bf16)
    keep = keep + swap(give, "core").astype(f32)
    keep = keep + swap(keep.astype(bf16), "zh").astype(f32)
    mine = jnp.maximum(keep + enc_bias[None, :], 0.0).astype(bf16)
    other = swap(mine, "core")
    return jnp.concatenate(
        [jnp.where(first, mine, other), jnp.where(first, other, mine)], axis=0
    )


def sum_all(value):
    axes = ("zh", "core", "y", "x", "z")
    copies = jnp.broadcast_to(value, (4 * SIDE**3, 128))
    terms = lax.all_to_all(copies, axes, split_axis=0, concat_axis=0, tiled=True)
    return jnp.sum(terms[:, 0])


def local(activations, enc_weight, enc_bias, dec_weight, dec_bias):
    rows = activations[0]
    chunks_a, chunks_b = gather_rows(rows)
    all_rows = jnp.concatenate(chunks_a + chunks_b, axis=0)
    token_count = all_rows.shape[0]
    partial_value = jnp.dot(all_rows, enc_weight[0], preferred_element_type=f32)
    w_dec = dec_weight[:, 0, :]
    layer_norm = jnp.sqrt(jnp.sum(jnp.square(w_dec.astype(f32)), axis=1) + 1e-06)
    latents = section_latents(partial_value, enc_bias)
    latent_sum = jnp.sum(latents.astype(f32), axis=0)
    penalty_part = penalty_weight / token_count * jnp.sum(latent_sum * layer_norm)
    coef = penalty_weight * latent_sum / token_count / layer_norm
    recon = jnp.dot(latents, w_dec, preferred_element_type=f32)
    size = token_count // 8
    chunks = [recon[size * i : size * i + size] for i in range(8)]
    recon_rows = scatter_rows(chunks[:4], chunks[4:])
    error_rows = recon_rows + dec_bias[0][None, :] - rows.astype(f32)
    square_sum = jnp.sum(error_rows * error_rows)
    loss = sum_all(square_sum / token_count + penalty_part)
    grad_rec = (2.0 * error_rows / token_count).astype(bf16)
    grads_a, grads_b = gather_rows(grad_rec)
    all_grads = jnp.concatenate(grads_a + grads_b, axis=0)
    place = (lax.axis_index("y") * SIDE + lax.axis_index("x")) * SIDE + lax.axis_index("z")
    width = all_grads.shape[1] // SIDE**3
    own = lax.dynamic_slice_in_dim(all_grads, place * width, width, axis=1)
    grad_bias = jnp.sum(own.astype(f32), axis=0, keepdims=True)
    grad_sum = lax.dot_general(
        latents, all_grads, (((0,), (0,)), ((), ())), preferred_element_type=f32
    )
    grad_dec = (grad_sum + coef[:, None] * w_dec.astype(f32)).astype(bf16)[:, None, :]
    return (loss, grad_dec, grad_bias)


def solution(mesh):
    grid = Mesh(
        mesh.devices.reshape(2, 2, SIDE, SIDE, SIDE), ("zh", "core", "y", "x", "z")
    )
    section, mp = ("zh", "core"), ("y", "x", "z")
    in_specs = (
        P(section, mp, None),
        P(section, None, mp),
        P(mp),
        P(mp, section, None),
        P(section, None),
    )
    out_specs = (P(), P(mp, section, None), P(section, mp))
    return jax.shard_map(local, mesh=grid, in_specs=in_specs, out_specs=out_specs, check_vma=False)
```

```python
import functools

import jax
import jax.numpy as jnp
from jax import lax
from jax.experimental import pallas as pl
from jax.experimental.pallas import tpu as pltpu
from jax.sharding import Mesh, PartitionSpec as P

penalty_weight = 2.0
SIDE = 4
bf16, f32 = jnp.bfloat16, jnp.float32
together = lax.optimization_barrier


def shift(value, axis, step):
    return lax.ppermute(value, axis, [(i, (i + step) % SIDE) for i in range(SIDE)])


def swap(value, axis):
    return lax.ppermute(value, axis, [(0, 1), (1, 0)])


def gather(value, axis):
    return [value] + [shift(value, axis, r) for r in range(1, SIDE)]


def exchange(blocks, axis):
    return [blocks[0]] + [shift(blocks[r].astype(bf16), axis, -r) for r in range(1, SIDE)]


def add_up(terms):
    total = terms[0]
    for term in terms[1:]:
        total = total + term.astype(f32)
    return total


def join(pieces, axis=0):
    return jnp.concatenate(pieces, axis=axis)


def stack_rows(pieces):
    size = pieces[0].shape[0]
    rows = size * len(pieces)
    low = jnp.array(-jnp.inf, pieces[0].dtype)
    padded = [
        lax.pad(piece, low, ((size * i, rows - size * (i + 1), 0), (0, 0, 0)))
        for i, piece in enumerate(pieces)
    ]
    return functools.reduce(jnp.maximum, padded)


def quarters(block):
    size = block.shape[0] // SIDE
    return [block[size * i : size * i + size] for i in range(SIDE)]


def gather_rows(rows):
    z = together(gather(rows, "z"))
    a, b = together((join(z[:2]), join(z[2:])))
    a, b = together((gather(a, "x"), gather(b, "y")))
    a, b = together((stack_rows(a), stack_rows(b)))
    pieces_b = gather(b, "x")
    later, pieces_b[1] = together((a, pieces_b[1]))
    pieces_a = [shift(later if r == 3 else a, "y", r) for r in range(1, SIDE)]
    return [a] + pieces_a, pieces_b


def opposite(chunks, axis):
    block = chunks[2].astype(bf16)
    half = block.shape[0] // 2
    return shift(block[:half], axis, -1), shift(block[half:], axis, 1)


def neighbours(chunks, passed, axis):
    half = chunks[2].shape[0] // 2
    before, after = chunks[1], chunks[3]
    before = join([before[:half] + passed[0].astype(f32), before[half:]])
    after = join([after[:half], after[half:] + passed[1].astype(f32)])
    return shift(before.astype(bf16), axis, -1), shift(after.astype(bf16), axis, 1)


def scatter_rows(chunks_a, chunks_b):
    passed = opposite(chunks_b, "x")
    a = exchange(chunks_a, "y")
    b = neighbours(chunks_b, passed, "x")
    a, b = together((add_up(a), add_up([chunks_b[0], *b])))
    a, b = together((exchange(quarters(a), "x"), exchange(quarters(b), "y")))
    a, b = together((add_up(a), add_up(b)))
    return together(exchange([a[:8], a[8:], b[:8], b[8:]], "z"))


def section_latents(part, enc_bias):
    half = part.shape[0] // 2
    first = lax.axis_index("core") == 0
    keep = jnp.where(first, part[:half], part[half:])
    give = jnp.where(first, part[half:], part[:half]).astype(bf16)
    keep = keep + swap(give, "core").astype(f32)
    keep = keep + swap(keep.astype(bf16), "zh").astype(f32)
    mine = jnp.maximum(keep + enc_bias[None, :], 0.0).astype(bf16)
    other = swap(mine, "core")
    return jnp.concatenate(
        [jnp.where(first, mine, other), jnp.where(first, other, mine)], axis=0
    )


def error_kernel(token_count, place, penalty, *refs):
    *terms, bias, rows, out = refs
    width = rows.shape[1]
    recon = add_up([term[...].astype(f32) for term in terms])
    error = recon + bias[...] - rows[...].astype(f32)
    out[:, :width] = (2.0 * error / token_count).astype(bf16)
    squares = jnp.sum(error * error, axis=1, keepdims=True)
    value = jnp.sum(squares, axis=0, keepdims=True) / token_count + penalty[0]
    high = value.astype(bf16).astype(f32)
    middle = (value - high).astype(bf16).astype(f32)
    low = value - high - middle
    shape = (rows.shape[0], 128)
    row = lax.broadcasted_iota(jnp.int32, shape, 0)
    column = lax.broadcasted_iota(jnp.int32, shape, 1)
    part = jnp.where(row == 0, high, jnp.where(row == 1, middle, low))
    out[:, width:] = jnp.where((column == place[0]) & (row < 3), part, 0.0).astype(bf16)


def error_rows(token_count, place, penalty, terms, bias, rows):
    shape = (rows.shape[0], rows.shape[1] + 128)
    scalar = pl.BlockSpec(memory_space=pltpu.SMEM)
    array = pl.BlockSpec(memory_space=pltpu.VMEM)
    return pl.pallas_call(
        functools.partial(error_kernel, token_count),
        out_shape=jax.ShapeDtypeStruct(shape, bf16),
        in_specs=[scalar] * 2 + [array] * (len(terms) + 2),
        out_specs=array,
        cost_estimate=pl.CostEstimate(flops=10 * rows.size, bytes_accessed=16 * rows.size, transcendentals=0),
        name="error_rows",
    )(place[None], penalty[None], *terms, bias, rows)


def sum_section(value):
    others = [
        lax.ppermute(value, ("zh", "core"), [(i, i ^ flip) for i in range(4)]) for flip in (1, 2, 3)
    ]
    return (value + others[0]) + (others[1] + others[2])


def local(activations, enc_weight, enc_bias, dec_weight, dec_bias):
    rows = activations[0]
    chunks_a, chunks_b = gather_rows(rows)
    all_rows = jnp.concatenate(chunks_a + chunks_b, axis=0)
    token_count = all_rows.shape[0]
    partial_value = jnp.dot(all_rows, enc_weight[0], preferred_element_type=f32)
    w_dec = dec_weight[:, 0, :]
    layer_norm = jnp.sqrt(jnp.sum(jnp.square(w_dec.astype(f32)), axis=1) + 1e-06)
    latents = section_latents(partial_value, enc_bias)
    latent_sum = jnp.sum(latents.astype(f32), axis=0)
    penalty_part = penalty_weight / token_count * jnp.sum(latent_sum * layer_norm)
    coef = penalty_weight * latent_sum / token_count / layer_norm
    recon = jnp.dot(latents, w_dec, preferred_element_type=f32)
    size = token_count // 8
    chunks = [recon[size * i : size * i + size] for i in range(8)]
    terms = scatter_rows(chunks[:4], chunks[4:])
    place = (lax.axis_index("y") * SIDE + lax.axis_index("x")) * SIDE + lax.axis_index("z")
    grad_rec = error_rows(token_count, place, penalty_part, terms, dec_bias, rows)
    width = rows.shape[1]
    grads_a, grads_b = gather_rows(grad_rec)
    pieces = grads_a + grads_b
    columns = sum(jnp.sum(piece[:, width:].astype(f32), axis=0) for piece in pieces)
    loss = sum_section(jnp.sum(columns, keepdims=True))[0]
    all_grads = join([piece[:, :width] for piece in pieces])
    width = width // SIDE**3
    own = lax.dynamic_slice_in_dim(all_grads, place * width, width, axis=1)
    grad_bias = jnp.sum(own.astype(f32), axis=0, keepdims=True)
    grad_sum = lax.dot_general(
        latents, all_grads, (((0,), (0,)), ((), ())), preferred_element_type=f32
    )
    grad_dec = (grad_sum + coef[:, None] * w_dec.astype(f32)).astype(bf16)[:, None, :]
    return (loss, grad_dec, grad_bias)


def solution(mesh):
    grid = Mesh(
        mesh.devices.reshape(2, 2, SIDE, SIDE, SIDE), ("zh", "core", "y", "x", "z")
    )
    section, mp = ("zh", "core"), ("y", "x", "z")
    in_specs = (
        P(section, mp, None),
        P(section, None, mp),
        P(mp),
        P(mp, section, None),
        P(section, None),
    )
    out_specs = (P(), P(mp, section, None), P(section, mp))
    return jax.shard_map(local, mesh=grid, in_specs=in_specs, out_specs=out_specs, check_vma=False)
```

```python
import functools

import jax
import jax.numpy as jnp
from jax import lax
from jax.experimental import pallas as pl
from jax.experimental.pallas import tpu as pltpu
from jax.sharding import Mesh, PartitionSpec as P

penalty_weight = 2.0
SIDE = 4
bf16, f32 = jnp.bfloat16, jnp.float32
together = lax.optimization_barrier


def shift(value, axis, step):
    return lax.ppermute(value, axis, [(i, (i + step) % SIDE) for i in range(SIDE)])


def swap(value, axis):
    return lax.ppermute(value, axis, [(0, 1), (1, 0)])


def gather(value, axis):
    return [value] + [shift(value, axis, r) for r in range(1, SIDE)]


def exchange(blocks, axis):
    return [blocks[0]] + [shift(blocks[r].astype(bf16), axis, -r) for r in range(1, SIDE)]


def add_up(terms):
    total = terms[0]
    for term in terms[1:]:
        total = total + term.astype(f32)
    return total


def join(pieces, axis=0):
    return jnp.concatenate(pieces, axis=axis)


def stack_rows(pieces):
    size = pieces[0].shape[0]
    rows = size * len(pieces)
    low = jnp.array(-jnp.inf, pieces[0].dtype)
    padded = [
        lax.pad(piece, low, ((size * i, rows - size * (i + 1), 0), (0, 0, 0)))
        for i, piece in enumerate(pieces)
    ]
    return functools.reduce(jnp.maximum, padded)


def quarters(block):
    size = block.shape[0] // SIDE
    return [block[size * i : size * i + size] for i in range(SIDE)]


def gather_rows(rows, paced):
    z = together(gather(rows, "z"))
    a, b = together((join(z[:2]), join(z[2:])))
    a, b = together((gather(a, "x"), gather(b, "y")))
    a, b = together((stack_rows(a), stack_rows(b)))
    pieces_b = gather(b, "x")
    later = a
    if paced:
        later, pieces_b[3] = together((a, pieces_b[3]))
    return [a] + [shift(later if r == 1 else a, "y", r) for r in range(1, SIDE)], pieces_b


def opposite(chunks, axis):
    block = chunks[2].astype(bf16)
    half = block.shape[0] // 2
    return shift(block[:half], axis, -1), shift(block[half:], axis, 1)


def neighbours(chunks, passed, axis):
    half = chunks[2].shape[0] // 2
    before, after = chunks[1], chunks[3]
    before = join([before[:half] + passed[0].astype(f32), before[half:]])
    after = join([after[:half], after[half:] + passed[1].astype(f32)])
    return shift(before.astype(bf16), axis, -1), shift(after.astype(bf16), axis, 1)


def scatter_rows(chunks_a, chunks_b):
    passed = opposite(chunks_b, "x")
    a = exchange(chunks_a, "y")
    b = neighbours(chunks_b, passed, "x")
    a, b = together((add_up(a), add_up([chunks_b[0], *b])))
    a, b = together((exchange(quarters(a), "x"), exchange(quarters(b), "y")))
    a, b = together((add_up(a), add_up(b)))
    return together(exchange([a[:8], a[8:], b[:8], b[8:]], "z"))


def section_latents(part, enc_bias):
    half = part.shape[0] // 2
    first = lax.axis_index("core") == 0
    keep = jnp.where(first, part[:half], part[half:])
    give = jnp.where(first, part[half:], part[:half]).astype(bf16)
    keep = keep + swap(give, "core").astype(f32)
    keep = keep + swap(keep.astype(bf16), "zh").astype(f32)
    mine = jnp.maximum(keep + enc_bias[None, :], 0.0).astype(bf16)
    other = swap(mine, "core")
    return jnp.concatenate(
        [jnp.where(first, mine, other), jnp.where(first, other, mine)], axis=0
    )


def error_kernel(token_count, place, penalty, *refs):
    *terms, bias, rows, out = refs
    width = rows.shape[1]
    recon = add_up([term[...].astype(f32) for term in terms])
    error = recon + bias[...] - rows[...].astype(f32)
    out[:, :width] = (2.0 * error / token_count).astype(bf16)
    squares = jnp.sum(error * error, axis=1, keepdims=True)
    value = jnp.sum(squares, axis=0, keepdims=True) / token_count + penalty[0]
    high = value.astype(bf16).astype(f32)
    middle = (value - high).astype(bf16).astype(f32)
    low = value - high - middle
    shape = (rows.shape[0], 128)
    row = lax.broadcasted_iota(jnp.int32, shape, 0)
    column = lax.broadcasted_iota(jnp.int32, shape, 1)
    part = jnp.where(row == 0, high, jnp.where(row == 1, middle, low))
    out[:, width:] = jnp.where((column == place[0]) & (row < 3), part, 0.0).astype(bf16)


def error_rows(token_count, place, penalty, terms, bias, rows):
    shape = (rows.shape[0], rows.shape[1] + 128)
    scalar = pl.BlockSpec(memory_space=pltpu.SMEM)
    array = pl.BlockSpec(memory_space=pltpu.VMEM)
    return pl.pallas_call(
        functools.partial(error_kernel, token_count),
        out_shape=jax.ShapeDtypeStruct(shape, bf16),
        in_specs=[scalar] * 2 + [array] * (len(terms) + 2),
        out_specs=array,
        cost_estimate=pl.CostEstimate(flops=10 * rows.size, bytes_accessed=16 * rows.size, transcendentals=0),
        name="error_rows",
    )(place[None], penalty[None], *terms, bias, rows)


def sum_section(value):
    others = [
        lax.ppermute(value, ("zh", "core"), [(i, i ^ flip) for i in range(4)]) for flip in (1, 2, 3)
    ]
    return (value + others[0]) + (others[1] + others[2])


def local(activations, enc_weight, enc_bias, dec_weight, dec_bias):
    rows = activations[0]
    chunks_a, chunks_b = gather_rows(rows, False)
    all_rows = jnp.concatenate(chunks_a + chunks_b, axis=0)
    token_count = all_rows.shape[0]
    partial_value = jnp.dot(all_rows, enc_weight[0], preferred_element_type=f32)
    w_dec = dec_weight[:, 0, :]
    layer_norm = jnp.sqrt(jnp.sum(jnp.square(w_dec.astype(f32)), axis=1) + 1e-06)
    latents = section_latents(partial_value, enc_bias)
    latent_sum = jnp.sum(latents.astype(f32), axis=0)
    penalty_part = penalty_weight / token_count * jnp.sum(latent_sum * layer_norm)
    coef = penalty_weight * latent_sum / token_count / layer_norm
    recon = jnp.dot(latents, w_dec, preferred_element_type=f32)
    size = token_count // 8
    chunks = [recon[size * i : size * i + size] for i in range(8)]
    terms = scatter_rows(chunks[:4], chunks[4:])
    place = (lax.axis_index("y") * SIDE + lax.axis_index("x")) * SIDE + lax.axis_index("z")
    grad_rec = error_rows(token_count, place, penalty_part, terms, dec_bias, rows)
    width = rows.shape[1]
    grads_a, grads_b = gather_rows(grad_rec, True)
    pieces = grads_a + grads_b
    columns = sum(jnp.sum(piece[:, width:].astype(f32), axis=0) for piece in pieces)
    loss = sum_section(jnp.sum(columns, keepdims=True))[0]
    all_grads = join([piece[:, :width] for piece in pieces])
    width = width // SIDE**3
    own = lax.dynamic_slice_in_dim(all_grads, place * width, width, axis=1)
    grad_bias = jnp.sum(own.astype(f32), axis=0, keepdims=True)
    grad_sum = lax.dot_general(
        latents, all_grads, (((0,), (0,)), ((), ())), preferred_element_type=f32
    )
    grad_dec = (grad_sum + coef[:, None] * w_dec.astype(f32)).astype(bf16)[:, None, :]
    return (loss, grad_dec, grad_bias)


def solution(mesh):
    grid = Mesh(
        mesh.devices.reshape(2, 2, SIDE, SIDE, SIDE), ("zh", "core", "y", "x", "z")
    )
    section, mp = ("zh", "core"), ("y", "x", "z")
    in_specs = (
        P(section, mp, None),
        P(section, None, mp),
        P(mp),
        P(mp, section, None),
        P(section, None),
    )
    out_specs = (P(), P(mp, section, None), P(section, mp))
    return jax.shard_map(local, mesh=grid, in_specs=in_specs, out_specs=out_specs, check_vma=False)
```

```python
import functools

import jax
import jax.numpy as jnp
from jax import lax
from jax.experimental import pallas as pl
from jax.experimental.pallas import tpu as pltpu
from jax.sharding import Mesh, PartitionSpec as P

penalty_weight = 2.0
SIDE = 4
bf16, f32 = jnp.bfloat16, jnp.float32
together = lax.optimization_barrier


def shift(value, axis, step):
    return lax.ppermute(value, axis, [(i, (i + step) % SIDE) for i in range(SIDE)])


def swap(value, axis):
    return lax.ppermute(value, axis, [(0, 1), (1, 0)])


def gather(value, axis):
    return [value] + [shift(value, axis, r) for r in range(1, SIDE)]


def exchange(blocks, axis):
    return [blocks[0]] + [shift(blocks[r].astype(bf16), axis, -r) for r in range(1, SIDE)]


def add_up(terms):
    total = terms[0]
    for term in terms[1:]:
        total = total + term.astype(f32)
    return total


def join(pieces, axis=0):
    return jnp.concatenate(pieces, axis=axis)


def stack_rows(pieces):
    size = pieces[0].shape[0]
    rows = size * len(pieces)
    low = jnp.array(-jnp.inf, pieces[0].dtype)
    padded = [
        lax.pad(piece, low, ((size * i, rows - size * (i + 1), 0), (0, 0, 0)))
        for i, piece in enumerate(pieces)
    ]
    return functools.reduce(jnp.maximum, padded)


def quarters(block):
    size = block.shape[0] // SIDE
    return [block[size * i : size * i + size] for i in range(SIDE)]


def gather_rows(rows, paced):
    z = together(gather(rows, "z"))
    a, b = together((join(z[:2]), join(z[2:])))
    a, b = together((gather(a, "x"), gather(b, "y")))
    a, b = together((stack_rows(a), stack_rows(b)))
    pieces_b = gather(b, "x")
    later = a
    if paced:
        later, pieces_b[3] = together((a, pieces_b[3]))
    return [a] + [shift(later if r == 1 else a, "y", r) for r in range(1, SIDE)], pieces_b


def opposite(chunks, axis):
    block = chunks[2].astype(bf16)
    half = block.shape[0] // 2
    return shift(block[:half], axis, -1), shift(block[half:], axis, 1)


def neighbours(chunks, passed, axis):
    half = chunks[2].shape[0] // 2
    before, after = chunks[1], chunks[3]
    before = join([before[:half] + passed[0].astype(f32), before[half:]])
    after = join([after[:half], after[half:] + passed[1].astype(f32)])
    return shift(before.astype(bf16), axis, -1), shift(after.astype(bf16), axis, 1)


def scatter_rows(chunks_a, chunks_b):
    passed = opposite(chunks_b, "x")
    a = exchange(chunks_a, "y")
    b = neighbours(chunks_b, passed, "x")
    a, b = together((add_up(a), add_up([chunks_b[0], *b])))
    a, b = together((exchange(quarters(a), "x"), exchange(quarters(b), "y")))
    a, b = together((add_up(a), add_up(b)))
    return together(exchange([a[:8], a[8:], b[:8], b[8:]], "z"))


def section_latents(part, enc_bias):
    half = part.shape[0] // 2
    first = lax.axis_index("core") == 0
    keep = jnp.where(first, part[:half], part[half:])
    give = jnp.where(first, part[half:], part[:half]).astype(bf16)
    keep = keep + swap(give, "core").astype(f32)
    keep = keep + swap(keep.astype(bf16), "zh").astype(f32)
    mine = jnp.maximum(keep + enc_bias[None, :], 0.0).astype(bf16)
    other = swap(mine, "core")
    return jnp.concatenate(
        [jnp.where(first, mine, other), jnp.where(first, other, mine)], axis=0
    )


def error_kernel(token_count, place, penalty, *refs):
    *terms, bias, rows, out = refs
    width = rows.shape[1]
    recon = add_up([term[...].astype(f32) for term in terms])
    error = recon + bias[...] - rows[...].astype(f32)
    out[:, :width] = (2.0 * error / token_count).astype(bf16)
    squares = jnp.sum(error * error, axis=1, keepdims=True)
    value = jnp.sum(squares, axis=0, keepdims=True) / token_count + penalty[0]
    high = value.astype(bf16).astype(f32)
    middle = (value - high).astype(bf16).astype(f32)
    low = value - high - middle
    shape = (rows.shape[0], 128)
    row = lax.broadcasted_iota(jnp.int32, shape, 0)
    column = lax.broadcasted_iota(jnp.int32, shape, 1)
    part = jnp.where(row == 0, high, jnp.where(row == 1, middle, low))
    out[:, width:] = jnp.where((column == place[0]) & (row < 3), part, 0.0).astype(bf16)


def error_rows(token_count, place, penalty, terms, bias, rows):
    shape = (rows.shape[0], rows.shape[1] + 128)
    scalar = pl.BlockSpec(memory_space=pltpu.SMEM)
    array = pl.BlockSpec(memory_space=pltpu.VMEM)
    return pl.pallas_call(
        functools.partial(error_kernel, token_count),
        out_shape=jax.ShapeDtypeStruct(shape, bf16),
        in_specs=[scalar] * 2 + [array] * (len(terms) + 2),
        out_specs=array,
        cost_estimate=pl.CostEstimate(flops=10 * rows.size, bytes_accessed=16 * rows.size, transcendentals=0),
        name="error_rows",
    )(place[None], penalty[None], *terms, bias, rows)


def local(activations, enc_weight, enc_bias, dec_weight, dec_bias):
    rows = activations[0]
    chunks_a, chunks_b = gather_rows(rows, False)
    all_rows = jnp.concatenate(chunks_a + chunks_b, axis=0)
    token_count = all_rows.shape[0]
    partial_value = jnp.dot(all_rows, enc_weight[0], preferred_element_type=f32)
    w_dec = dec_weight[:, 0, :]
    layer_norm = jnp.sqrt(jnp.sum(jnp.square(w_dec.astype(f32)), axis=1) + 1e-06)
    latents = section_latents(partial_value, enc_bias)
    latent_sum = jnp.sum(latents.astype(f32), axis=0)
    penalty_part = penalty_weight / token_count * jnp.sum(latent_sum * layer_norm)
    coef = penalty_weight * latent_sum / token_count / layer_norm
    recon = jnp.dot(latents, w_dec, preferred_element_type=f32)
    size = token_count // 8
    chunks = [recon[size * i : size * i + size] for i in range(8)]
    terms = scatter_rows(chunks[:4], chunks[4:])
    place = (lax.axis_index("y") * SIDE + lax.axis_index("x")) * SIDE + lax.axis_index("z")
    grad_rec = error_rows(token_count, place, penalty_part, terms, dec_bias, rows)
    width = rows.shape[1]
    grads_a, grads_b = gather_rows(grad_rec, True)
    pieces = grads_a + grads_b
    columns = sum(jnp.sum(piece[:, width:].astype(f32), axis=0) for piece in pieces)
    all_grads = join([piece[:, :width] for piece in pieces])
    total, all_grads = together((jnp.sum(columns, keepdims=True), all_grads))
    total = total + swap(total, "zh")
    bias_grads, total = together((all_grads, total))
    loss = (total + swap(total, "core"))[0]
    width = width // SIDE**3
    own = lax.dynamic_slice_in_dim(bias_grads, place * width, width, axis=1)
    grad_bias = jnp.sum(own.astype(f32), axis=0, keepdims=True)
    grad_sum = lax.dot_general(
        latents, all_grads, (((0,), (0,)), ((), ())), preferred_element_type=f32
    )
    grad_dec = (grad_sum + coef[:, None] * w_dec.astype(f32)).astype(bf16)[:, None, :]
    return (loss, grad_dec, grad_bias)


def solution(mesh):
    grid = Mesh(
        mesh.devices.reshape(2, 2, SIDE, SIDE, SIDE), ("zh", "core", "y", "x", "z")
    )
    section, mp = ("zh", "core"), ("y", "x", "z")
    in_specs = (
        P(section, mp, None),
        P(section, None, mp),
        P(mp),
        P(mp, section, None),
        P(section, None),
    )
    out_specs = (P(), P(mp, section, None), P(section, mp))
    return jax.shard_map(local, mesh=grid, in_specs=in_specs, out_specs=out_specs, check_vma=False)
```
